32 devices in a mesh: grp: 2 (over y), row: 8 (over z, x), layer: 2 (over core).
Axes of the slice: x: 2, y: 2, z: 4, core: 2. Of those that a mesh axis runs over, the one named last changes fastest.
Arguments:
- train_codes: bfloat16 [8192, 2, 4096], P(('grp', 'row'), 'layer'), parts along dimension 0, may hold values from -4 to 4
- block_scales: float32 [8192, 2, 32], P(('grp', 'row'), 'layer'), parts along dimension 0, may hold values from 0.0004 to 0.004
- queries: bfloat16 [512, 2, 4096], P('row', 'layer'), may hold values from -6 to 6
- left_factor: float32 [2, 64, 64], P('layer'), may hold values from -1 to 5, as said below
- right_factor: float32 [2, 64, 64], P('layer'), may hold values from -1 to 5, as said below
Outputs:
- influence: float32 [8192, 512], P(('grp', 'row', 'layer')), parts along dimension 0
The draws below stay inside these ranges and needn't reach their ends.
There are 2 independent parts, one for each index of `grp`. The reference program is written for one: setup_inputs(seed, part) draws one part's arguments, and reference() takes and returns one part's arrays. A program takes and returns all parts, laid end to end along the dimension named above; an argument that names none is the same for every part. Nothing has to cross between parts.
Inputs may be any that keep to these rules, and one draw needn't show every extreme that they name: `left_factor`: symmetric. `right_factor`: symmetric.
All inputs are finite; a program needn't handle non-finite values.
Results may differ from the reference program's by a relative error of at most 0.004.
Values may be sent and summed in bfloat16 or wider, within the bound.
A program may use at most 64 MiB of HBM per device.

```python
import math
import jax
import jax.numpy as jnp
from jax import lax

KO = 64
KI = 64
Q = 512
DIM = 4096
NBLK = 32
LAYERS = 2
ROWS = 4096


def factor_draw(key, layers, order, low, high):
    diag_key, off_key = jax.random.split(key)
    diagonal = jax.random.uniform(diag_key, (layers, order), jnp.float32, low, high)
    noise = jax.random.normal(off_key, (layers, order, order), jnp.float32) * (0.7 / order ** 0.5)
    noise = jnp.clip(noise, -0.45, 0.45)
    symmetric = (noise + jnp.swapaxes(noise, 1, 2)) * 0.7071
    return symmetric + jnp.eye(order, dtype=jnp.float32)[None] * diagonal[:, :, None]


def draw_left_factor(key, part):
    key = jax.random.fold_in(key, 11)
    return factor_draw(key, LAYERS, KO, 2.0, 4.0)


def draw_right_factor(key, part):
    key = jax.random.fold_in(key, 23)
    return factor_draw(key, LAYERS, KI, 2.0, 4.0)


def block_scale(rng, extent, cuts, smallest, largest):
    def one(axis_at, parts):
        draws = jax.random.uniform(jax.random.fold_in(jax.random.fold_in(rng, 6), axis_at), (parts,), jnp.float32, smallest / len(cuts), largest / len(cuts))
        return jnp.repeat(jnp.exp(draws), extent[axis_at] // parts).reshape((-1,) + (1,) * (len(extent) - axis_at - 1))

    level = one(*cuts[0])
    for cut in cuts[1:]:
        level = level * one(*cut)
    return level


def bell_draw(key, extent, deviation, most, pieces=(), held_as=jnp.bfloat16):
    values = deviation * jax.random.normal(key, extent, jnp.float32)
    if pieces:
        values = values * block_scale(key, extent, pieces, -0.22, 0.18)
    return jnp.clip(values, -most, most).astype(held_as)


def setup_inputs(seed: int = 0, part: int = 0) -> dict:
    streams_of = jax.random.split(jax.random.key(seed), 6)
    part_keys = jax.random.split(jax.random.fold_in(streams_of[5], part), 6)
    train_codes = bell_draw(part_keys[0], (ROWS, LAYERS, DIM), 1.0, 4.0, ((0, 8), (1, 2)))
    block_scales = jnp.clip(jnp.exp(math.log(0.004) - 2.3025852 * jax.random.uniform(part_keys[1], (ROWS, LAYERS, NBLK), jnp.float32) ** block_scale(part_keys[1], (ROWS, LAYERS, NBLK), ((0, 8), (1, 2)), -0.2, 0.2)), 0.0004, 0.004)
    queries = bell_draw(streams_of[2], (Q, LAYERS, DIM), 1.0, 6.0, ((0, 8), (1, 2)))
    left_factor = draw_left_factor(jax.random.fold_in(streams_of[5], 71), part)
    right_factor = draw_right_factor(jax.random.fold_in(streams_of[5], 71), part)
    return dict(train_codes=train_codes, block_scales=block_scales, queries=queries, left_factor=left_factor, right_factor=right_factor)


def precondition(flat, left_factor, right_factor):
    count = flat.shape[0]
    layers = left_factor.shape[0]
    outer = left_factor.shape[1]
    inner = right_factor.shape[1]
    blocks = flat.reshape(count, layers, outer, inner).astype(jnp.float32)
    result = jnp.einsum("lab,nlbc,lcd->nlad", left_factor.astype(jnp.float32), blocks, right_factor.astype(jnp.float32), precision=lax.Precision.HIGHEST)
    return result.astype(jnp.bfloat16).reshape(count, layers * outer * inner)


def reference(train_codes, block_scales, queries, left_factor, right_factor):
    rows_all = train_codes.shape[0]
    layers = train_codes.shape[1]
    width = train_codes.shape[2]
    blocks = block_scales.shape[2]
    prepared = precondition(queries.reshape(Q, layers * width), left_factor, right_factor)
    step_rows = math.gcd(rows_all, 4096)

    def score_block(index):
        start = (index * step_rows).astype(jnp.int32)
        codes = lax.dynamic_slice_in_dim(train_codes, start, step_rows, 0)
        scales = lax.dynamic_slice_in_dim(block_scales, start, step_rows, 0)
        values = codes.reshape(step_rows, layers, blocks, width // blocks).astype(jnp.float32) * scales[..., None]
        dequant = values.astype(jnp.bfloat16).reshape(step_rows, layers * width)
        return jnp.dot(dequant, prepared.T, preferred_element_type=jnp.float32)

    scored = lax.map(score_block, jnp.arange(rows_all // step_rows, dtype=jnp.int32))
    return scored.reshape(rows_all, Q)
```

```python
import functools

import jax
import jax.numpy as jnp
from jax import lax
from jax.experimental import pallas as pl
from jax.experimental.pallas import tpu as pltpu
from jax.sharding import PartitionSpec as P

MESH = pl.DeviceIdType.MESH
PLANES = 4
CHUNKS = 4
EVENTS = (PLANES - 1) * CHUNKS


def split(value):
    high = value.astype(jnp.bfloat16)
    return high, (value - high.astype(jnp.float32)).astype(jnp.bfloat16)


def dot(a, b):
    return jnp.dot(a, b, preferred_element_type=jnp.float32)


def score_kernel(
    codes_hbm, scales_ref, queries_ref, left_ref, right_ref, out_ref,
    codes, train, scales, prepared, spread, mixed, left_diag, right_diag, mine, theirs,
    codes_sem, recv_sem, up_sem, down_sem, x_sem, y_sem, part_sem, part_recv_sem,
):
    rows, width = codes.shape
    order = left_ref.shape[0]
    count = queries_ref.shape[0]
    step = count // CHUNKS
    half = rows // 2
    y, at, layer = lax.axis_index("grp"), lax.axis_index("row"), lax.axis_index("layer")
    z, x = at // 2, at % 2
    middle = (z * (PLANES - 1 - z)) // 2
    sign = 1 - 2 * (z // 2)
    above = {"row": at + 2}
    below = {"row": at - 2}
    beside = {"row": at + 1 - 2 * x}
    across = {"grp": 1 - y}
    core = {"layer": 1 - layer}

    barrier = pltpu.get_barrier_semaphore()
    for where in (beside, across, core):
        pl.semaphore_signal(barrier, inc=1, device_id=where, device_id_type=MESH)

    @pl.when(z > 0)
    def _():
        pl.semaphore_signal(barrier, inc=1, device_id=below, device_id_type=MESH)

    @pl.when(z < PLANES - 1)
    def _():
        pl.semaphore_signal(barrier, inc=1, device_id=above, device_id_type=MESH)

    fetch = pltpu.make_async_copy(codes_hbm, codes, codes_sem)
    fetch.start()

    def plane_of(k):
        step_end = k
        step_middle = (-1, 1, 2)[k - 1]
        return z + sign * (step_end + middle * (step_middle - step_end))

    def piece(plane, side, c):
        start = pl.multiple_of((plane * 2 + side) * count + c * step, step)
        return prepared.at[pl.ds(start, step), :]

    def hop(plane, side, c, send_sem, where):
        block = piece(plane, side, c)
        return pltpu.make_async_remote_copy(
            src_ref=block, dst_ref=block, send_sem=send_sem, recv_sem=recv_sem.at[plane * 2 + side, c],
            device_id=where, device_id_type=MESH,
        )

    def up(plane, c):
        return hop(plane, x, c, up_sem.at[plane, c], above)

    def down(plane, c):
        return hop(plane, x, c, down_sem.at[plane, c], below)

    def over_x(plane, c):
        return hop(plane, x, c, x_sem.at[plane, c], beside)

    def over_y(plane, c):
        return hop(plane, 1 - x, c, y_sem.at[plane, c], across)

    def landed(plane, side, c):
        hop(plane, side, c, up_sem.at[0, 0], beside).wait_recv()

    for ref, diag in ((right_ref, right_diag), (left_ref, left_diag)):
        tall = jnp.concatenate([ref[...]] * 4, axis=0)
        wide = jnp.concatenate([jnp.concatenate([tall, tall], axis=1)] * 2, axis=1)
        row_at = lax.broadcasted_iota(jnp.int32, wide.shape, 0) // order
        col_at = lax.broadcasted_iota(jnp.int32, wide.shape, 1) // order
        high, low = split(jnp.where(row_at == col_at, wide, 0.0))
        diag[0] = high
        diag[1] = low

    lane = lax.broadcasted_iota(jnp.int32, (step, 128), 1)

    def prepare(c):
        piece_of = queries_ref[c * step : (c + 1) * step, :]
        groups = width // 256
        stacked = jnp.concatenate([piece_of[:, g * 256 : (g + 1) * 256] for g in range(groups)], axis=0)
        result = dot(stacked, right_diag[0]) + dot(stacked, right_diag[1])
        for pair in range(width // 128):
            g, h = pair // 2, pair % 2
            value = result[g * step : (g + 1) * step, h * 128 : (h + 1) * 128]
            spread[pl.ds(2 * pair, step, stride=order), :] = value
            spread[pl.ds(2 * pair + 1, step, stride=order), :] = pltpu.roll(value, 64, 1)
        for i in range(step // 4):
            high, low = split(spread[i * 256 : (i + 1) * 256, :])
            mixed[i * 256 : (i + 1) * 256, :] = (
                dot(left_diag[0], high) + dot(left_diag[1], high) + dot(left_diag[0], low)
            )
        start = pl.multiple_of(at * count + c * step, step)
        for pair in range(width // 128):
            even = mixed[pl.ds(2 * pair, step, stride=order), :]
            odd = pltpu.roll(mixed[pl.ds(2 * pair + 1, step, stride=order), :], 64, 1)
            prepared[pl.ds(start, step), pair * 128 : (pair + 1) * 128] = jnp.where(
                lane < 64, even, odd
            ).astype(jnp.bfloat16)

    def spread_out(plane, c):
        @pl.when(c % 2 == y)
        def _():
            over_x(plane, c).start()

    def relay_y(plane, c):
        @pl.when(c % 2 == y)
        def _():
            landed(plane, 1 - x, c)
            over_y(plane, c).start()

    def finish_y(plane):
        for c in range(CHUNKS):
            @pl.when(c % 2 != y)
            def _():
                landed(plane, 1 - x, c)

    def exchange(plane):
        return pltpu.make_async_remote_copy(
            src_ref=mine.at[plane, 1 - layer], dst_ref=theirs.at[plane],
            send_sem=part_sem.at[plane], recv_sem=part_recv_sem.at[plane],
            device_id=core, device_id_type=MESH,
        )

    def score(plane):
        start = pl.multiple_of(plane * 2 * count, 2 * count)
        for h in range(2):
            mine[plane, h] = lax.dot_general(
                train[h * half : (h + 1) * half, :], prepared[pl.ds(start, 2 * count), :],
                (((1,), (1,)), ((), ())), preferred_element_type=jnp.float32,
            )
        exchange(plane).start()

    def dequantize():
        @pl.loop(0, rows // 64)
        def _(t):
            span = pl.ds(pl.multiple_of(t * 64, 64), 64)
            for j in range(width // 128):
                train[span, j * 128 : (j + 1) * 128] = (
                    codes[span, j * 128 : (j + 1) * 128].astype(jnp.float32) * scales[span, j : j + 1]
                ).astype(jnp.bfloat16)

    for c in range(CHUNKS):
        prepare(c)
        if c == 0:
            pl.semaphore_wait(barrier, 3 + jnp.minimum(z, 1) + jnp.minimum(PLANES - 1 - z, 1))

        @pl.when(z < PLANES - 1)
        def _():
            up(z, c).start()

        @pl.when(z > 0)
        def _():
            down(z, c).start()

        spread_out(z, c)

    fetch.wait()
    scales[...] = scales_ref[...].T
    relay_y(z, 0)
    relay_y(z, 1)
    dequantize()
    relay_y(z, 2)
    relay_y(z, 3)

    def event(e):
        k_end, c_end = 1 + e // CHUNKS, e % CHUNKS
        if e < 2 * CHUNKS:
            k_mid, c_mid = 1 + e % 2, e // 2
        else:
            k_mid, c_mid = k_end, c_end
        plane = plane_of(k_end) + middle * (plane_of(k_mid) - plane_of(k_end))
        return plane, c_end + middle * (c_mid - c_end)

    for e in range(EVENTS):
        plane, c = event(e)
        landed(plane, x, c)

        @pl.when((plane < z) & (z < PLANES - 1))
        def _():
            up(plane, c).start()

        @pl.when((plane > z) & (z > 0))
        def _():
            down(plane, c).start()

        spread_out(plane, c)
        if e >= 2:
            relay_y(*event(e - 2))
        if e == 3:
            finish_y(z)
            score(z)
        if e == EVENTS - 2:
            first = plane_of(1)
            finish_y(first)
            score(first)
    relay_y(*event(EVENTS - 2))
    relay_y(*event(EVENTS - 1))
    for k in (2, 3):
        plane = plane_of(k)
        finish_y(plane)
        score(plane)

    for plane in [z] + [plane_of(k) for k in (1, 2, 3)]:
        exchange(plane).wait()
        start = pl.multiple_of(plane * 2 * count, 2 * count)
        out_ref[:, pl.ds(start, 2 * count)] = mine[plane, layer] + theirs[plane]

    for plane in range(PLANES):
        for c in range(CHUNKS):
            @pl.when((plane <= z) & (z < PLANES - 1))
            def _():
                up(plane, c).wait_send()

            @pl.when((plane >= z) & (z > 0))
            def _():
                down(plane, c).wait_send()

            @pl.when(c % 2 == y)
            def _():
                over_x(plane, c).wait_send()
                over_y(plane, c).wait_send()


def per_device_kernel(train_codes, block_scales, queries, left_factor, right_factor):
    rows, _, width = train_codes.shape
    count = queries.shape[0]
    order = left_factor.shape[1]
    step = count // CHUNKS
    blocks = block_scales.shape[2]
    total = 2 * PLANES * count
    vmem = pl.BlockSpec(memory_space=pltpu.VMEM)
    return pl.pallas_call(
        score_kernel,
        out_shape=jax.ShapeDtypeStruct((rows // 2, total), jnp.float32),
        in_specs=[pl.BlockSpec(memory_space=pl.ANY)] + [vmem] * 4,
        out_specs=vmem,
        scratch_shapes=[
            pltpu.VMEM((rows, width), jnp.bfloat16),
            pltpu.VMEM((rows, width), jnp.bfloat16),
            pltpu.VMEM((rows, blocks), jnp.float32),
            pltpu.VMEM((total, width), jnp.bfloat16),
            pltpu.VMEM((step * order, 128), jnp.float32),
            pltpu.VMEM((step * order, 128), jnp.float32),
            pltpu.VMEM((2, 4 * order, 4 * order), jnp.bfloat16),
            pltpu.VMEM((2, 4 * order, 4 * order), jnp.bfloat16),
            pltpu.VMEM((PLANES, 2, rows // 2, 2 * count), jnp.float32),
            pltpu.VMEM((PLANES, rows // 2, 2 * count), jnp.float32),
            pltpu.SemaphoreType.DMA,
            pltpu.SemaphoreType.DMA((2 * PLANES, CHUNKS)),
            pltpu.SemaphoreType.DMA((PLANES, CHUNKS)),
            pltpu.SemaphoreType.DMA((PLANES, CHUNKS)),
            pltpu.SemaphoreType.DMA((PLANES, CHUNKS)),
            pltpu.SemaphoreType.DMA((PLANES, CHUNKS)),
            pltpu.SemaphoreType.DMA((PLANES,)),
            pltpu.SemaphoreType.DMA((PLANES,)),
        ],
        compiler_params=pltpu.CompilerParams(
            collective_id=0, has_side_effects=True, vmem_limit_bytes=40 * 1024 * 1024
        ),
        cost_estimate=pl.CostEstimate(
            flops=2 * rows * total * width, bytes_accessed=2 * rows * width, transcendentals=0
        ),
        name="score_kernel",
    )(
        train_codes.reshape(rows, width),
        block_scales.reshape(rows, blocks).T,
        queries.reshape(count, width),
        left_factor[0],
        right_factor[0],
    )

def precondition(flat, left_factor, right_factor):
    count = flat.shape[0]
    layers = left_factor.shape[0]
    outer = left_factor.shape[1]
    inner = right_factor.shape[1]
    blocks = flat.reshape(count, layers, outer, inner).astype(jnp.float32)
    result = jnp.einsum(
        "lab,nlbc,lcd->nlad", left_factor, blocks, right_factor, precision=lax.Precision.HIGHEST
    )
    return result.astype(jnp.bfloat16).reshape(count, layers * outer * inner)


def per_device(train_codes, block_scales, queries, left_factor, right_factor):
    rows, layers, width = train_codes.shape
    blocks = block_scales.shape[2]
    values = (
        train_codes.reshape(rows, layers, blocks, width // blocks).astype(jnp.float32)
        * block_scales[..., None]
    )
    dequant = values.astype(jnp.bfloat16).reshape(rows, layers * width)
    flat = queries.reshape(queries.shape[0], layers * width)
    sending = precondition(flat, left_factor, right_factor)
    partial_scores = jnp.einsum(
        "rk,qk->rq",
        dequant,
        lax.all_gather(sending, "row", axis=0, tiled=True),
        preferred_element_type=jnp.float32,
    )
    return lax.psum_scatter(partial_scores, "layer", scatter_dimension=0, tiled=True)


def solution(mesh):
    small = mesh.shape["grp"] == 2 and mesh.shape["row"] == 2 * PLANES and mesh.shape["layer"] == 2
    return jax.shard_map(
        per_device_kernel if small else per_device,
        mesh=mesh,
        in_specs=(
            P(("grp", "row"), "layer", None),
            P(("grp", "row"), "layer", None),
            P("row", "layer", None),
            P("layer", None, None),
            P("layer", None, None),
        ),
        out_specs=P(("grp", "row", "layer"), None),
        check_vma=False,
    )
```

```python
import jax
import jax.numpy as jnp
from jax import lax
from jax.experimental import pallas as pl
from jax.experimental.pallas import tpu as pltpu
from jax.sharding import PartitionSpec as P

MESH = pl.DeviceIdType.MESH
PLANES = 4
GROUPS = 4
SINGLE = 2
LAG = 4
AHEAD = 4
CARRIED = [(g, other) for g in range(GROUPS) for other in range(2) if not (other and g < SINGLE)]


def split(value):
    high = value.astype(jnp.bfloat16)
    return high, (value - high.astype(jnp.float32)).astype(jnp.bfloat16)


def dot(a, b):
    return jnp.dot(a, b, preferred_element_type=jnp.float32)


def score_kernel(
    codes_hbm, scales_hbm, queries_hbm, left_hbm, right_hbm, out_hbm,
    codes, train, flat_scales, scales, queries, left, right, prepared, spread, mixed,
    left_diag, right_diag, mine, theirs, result,
    fetch_sem, query_sem, out_sem, recv_sem, up_sem, down_sem, x_sem, relay_sem, y_sem, part_sem, part_recv_sem,
):
    rows, width = codes.shape
    order = left.shape[0]
    count = queries.shape[0]
    step = count // GROUPS
    half = rows // 2
    y, at, layer = lax.axis_index("grp"), lax.axis_index("row"), lax.axis_index("layer")
    z, x = at // 2, at % 2
    middle = (z * (PLANES - 1 - z)) // 2
    sign = 1 - 2 * (z // 2)
    above = {"row": at + 2}
    below = {"row": at - 2}
    beside = {"row": at + 1 - 2 * x}
    across = {"grp": 1 - y}
    core = {"layer": 1 - layer}

    barrier = pltpu.get_barrier_semaphore()
    for where in (beside, across, core):
        pl.semaphore_signal(barrier, inc=1, device_id=where, device_id_type=MESH)

    @pl.when(z > 0)
    def _():
        pl.semaphore_signal(barrier, inc=1, device_id=below, device_id_type=MESH)

    @pl.when(z < PLANES - 1)
    def _():
        pl.semaphore_signal(barrier, inc=1, device_id=above, device_id_type=MESH)

    def fetch_queries(g):
        span = pl.ds(g * step, step)
        return pltpu.make_async_copy(queries_hbm.at[span, :], queries.at[span, :], query_sem.at[g])

    fetch_left = pltpu.make_async_copy(left_hbm, left, fetch_sem.at[0])
    fetch_right = pltpu.make_async_copy(right_hbm, right, fetch_sem.at[1])
    fetch_scales = pltpu.make_async_copy(scales_hbm, flat_scales, fetch_sem.at[2])
    fetch_codes = pltpu.make_async_copy(codes_hbm, codes, fetch_sem.at[3])
    fetch_right.start()
    fetch_left.start()
    for g in range(GROUPS):
        fetch_queries(g).start()
    fetch_scales.start()
    fetch_codes.start()

    def plane_of(k):
        step_middle = (1, -1, 2)[k - 1]
        return z + sign * (k + middle * (step_middle - k))

    def half_of(other):
        return y + other * (1 - 2 * y)

    def piece(plane, side, g, h):
        start = pl.multiple_of((plane * 2 + side) * count + g * step, step)
        return prepared.at[pl.ds(start, step), pl.ds(pl.multiple_of(h * (width // 2), width // 2), width // 2)]

    def hop(plane, side, g, other, send_sem, where):
        h = half_of(other)
        block = piece(plane, side, g, h)
        return pltpu.make_async_remote_copy(
            src_ref=block, dst_ref=block, send_sem=send_sem, recv_sem=recv_sem.at[plane * 2 + side, 2 * g + h],
            device_id=where, device_id_type=MESH,
        )

    def up(plane, g, other):
        return hop(plane, x, g, other, up_sem.at[plane, 2 * g + other], above)

    def down(plane, g, other):
        return hop(plane, x, g, other, down_sem.at[plane, 2 * g + other], below)

    def over_x(plane, g, other):
        return hop(plane, x, g, other, x_sem.at[plane, 2 * g + other], beside)

    def over_y(plane, g):
        return hop(plane, x, g, 0, y_sem.at[plane, g], across)

    def relayed(plane, g):
        return hop(plane, 1 - x, g, 0, relay_sem.at[plane, g], across)

    def landed(plane, side, g, other):
        hop(plane, side, g, other, up_sem.at[0, 0], beside).wait_recv()

    def fill_diag(ref, diag):
        tall = jnp.concatenate([ref[...]] * 4, axis=0)
        wide = jnp.concatenate([jnp.concatenate([tall, tall], axis=1)] * 2, axis=1)
        row_at = lax.broadcasted_iota(jnp.int32, wide.shape, 0) // order
        col_at = lax.broadcasted_iota(jnp.int32, wide.shape, 1) // order
        high, low = split(jnp.where(row_at == col_at, wide, 0.0))
        diag[0] = high
        diag[1] = low

    lane = lax.broadcasted_iota(jnp.int32, (step, 128), 1)

    def prepare(c):
        fetch_queries(c).wait()
        piece_of = queries[c * step : (c + 1) * step, :]
        stacked = jnp.concatenate([piece_of[:, g * 256 : (g + 1) * 256] for g in range(width // 256)], axis=0)
        turned = dot(stacked, right_diag[0]) + dot(stacked, right_diag[1])
        for pair in range(width // 128):
            g, h = pair // 2, pair % 2
            value = turned[g * step : (g + 1) * step, h * 128 : (h + 1) * 128]
            spread[pl.ds(2 * pair, step, stride=order), :] = value
            spread[pl.ds(2 * pair + 1, step, stride=order), :] = pltpu.roll(value, 64, 1)
        for i in range(step // 4):
            high, low = split(spread[i * 256 : (i + 1) * 256, :])
            mixed[i * 256 : (i + 1) * 256, :] = (
                dot(left_diag[0], high) + dot(left_diag[1], high) + dot(left_diag[0], low)
            )
        start = pl.multiple_of(at * count + c * step, step)
        for pair in range(width // 128):
            even = mixed[pl.ds(2 * pair, step, stride=order), :]
            odd = pltpu.roll(mixed[pl.ds(2 * pair + 1, step, stride=order), :], 64, 1)
            prepared[pl.ds(start, step), pair * 128 : (pair + 1) * 128] = jnp.where(
                lane < 64, even, odd
            ).astype(jnp.bfloat16)

    def relay(plane, g):
        landed(plane, 1 - x, g, 0)
        relayed(plane, g).start()

    def finish_own():
        landed(z, 1 - x, 0, 1)
        for g in range(1, GROUPS):
            landed(z, 1 - x, g, 0)
            landed(z, 1 - x, g, 1)

    def finish(plane):
        for g in range(GROUPS):
            if g < SINGLE:
                landed(plane, x, g, 1)
            landed(plane, 1 - x, g, 1)

    def exchange(plane):
        return pltpu.make_async_remote_copy(
            src_ref=mine.at[plane, 1 - layer], dst_ref=theirs.at[plane],
            send_sem=part_sem.at[plane], recv_sem=part_recv_sem.at[plane],
            device_id=core, device_id_type=MESH,
        )

    def score(plane):
        start = pl.multiple_of(plane * 2 * count, 2 * count)
        for h in range(2):
            mine[plane, h] = lax.dot_general(
                train[h * half : (h + 1) * half, :], prepared[pl.ds(start, 2 * count), :],
                (((1,), (1,)), ((), ())), preferred_element_type=jnp.float32,
            )
        exchange(plane).start()

    def give(plane):
        start = pl.multiple_of(plane * 2 * count, 2 * count)
        return pltpu.make_async_copy(result.at[plane], out_hbm.at[:, pl.ds(start, 2 * count)], out_sem.at[plane])

    def combine(plane):
        exchange(plane).wait()
        result[plane] = mine[plane, layer] + theirs[plane]
        give(plane).start()

    def dequantize(part):
        @pl.loop(0, rows // (64 * GROUPS))
        def _(t):
            span = pl.ds(pl.multiple_of(part * (rows // GROUPS) + t * 64, 64), 64)
            for j in range(width // 128):
                train[span, j * 128 : (j + 1) * 128] = (
                    codes[span, j * 128 : (j + 1) * 128].astype(jnp.float32) * scales[span, j : j + 1]
                ).astype(jnp.bfloat16)

    fetch_right.wait()
    fill_diag(right, right_diag)
    fetch_left.wait()
    fill_diag(left, left_diag)
    def send_own(g, other):
        @pl.when(z < PLANES - 1)
        def _():
            up(z, g, other).start()

        @pl.when(z > 0)
        def _():
            down(z, g, other).start()

    def outward(plane, g, other):
        @pl.when(z == 1)
        def _():
            down(plane, g, other).start()

        @pl.when(z == 2)
        def _():
            up(plane, g, other).start()

    def inward(plane, g, other):
        @pl.when(z == 1)
        def _():
            up(plane, g, other).start()

        @pl.when(z == 2)
        def _():
            down(plane, g, other).start()

    later = []
    for g in range(GROUPS):
        prepare(g)
        if g == 0:
            pl.semaphore_wait(barrier, 3 + jnp.minimum(z, 1) + jnp.minimum(PLANES - 1 - z, 1))
        for row_group, other in CARRIED[:AHEAD]:
            if row_group == g:
                send_own(g, other)
        if g == 0:
            over_x(z, 0, 0).start()
        elif g == 1:
            over_x(z, 1, 0).start()
            over_x(z, 1, 1).start()
        else:
            later += [(g, 0), (g, 1)]

    fetch_scales.wait()
    scales[...] = flat_scales[...].T
    fetch_codes.wait()
    relay(z, 0)

    events = [(k, g, other) for k in (1, 2, 3) for g, other in CARRIED]
    relays = {}
    for e, (k, g, other) in enumerate(events):
        if not other:
            relays.setdefault(e + LAG, []).append((k, g))
    for e, (k, g, other) in enumerate(events):
        plane = plane_of(k)
        if k == 1:
            landed(plane, x, g, other)
        else:
            @pl.when(middle == 0)
            def _():
                landed(plane, x, g, other)

        due = e + AHEAD
        each = len(CARRIED)
        if due < each:
            send_own(*CARRIED[due])
        elif due < 2 * each:
            due_piece = CARRIED[due - each]

            @pl.when(middle == 1)
            def _():
                outward(plane_of(1), *due_piece)
                landed(plane_of(2), x, *due_piece)
                inward(plane_of(2), *due_piece)
        elif due < 3 * each:
            due_piece = CARRIED[due - 2 * each]

            @pl.when(middle == 1)
            def _():
                landed(plane_of(3), x, *due_piece)
                outward(plane_of(3), *due_piece)

        if other:
            if later:
                over_x(z, *later.pop(0)).start()
        else:
            over_x(plane, g, 0).start()
            if g < SINGLE:
                over_y(plane, g).start()
        for late_k, late_g in relays.pop(e, []):
            relay(plane_of(late_k), late_g)
        if e in (1, 3, 5, 7):
            dequantize(e // 2)
        if e == 13:
            finish_own()
            score(z)
        if e == 15:
            finish(plane_of(1))
            score(plane_of(1))
    for e in sorted(relays):
        for late_k, late_g in relays[e]:
            relay(plane_of(late_k), late_g)
    finish(plane_of(2))
    score(plane_of(2))
    combine(z)
    combine(plane_of(1))
    finish(plane_of(3))
    score(plane_of(3))
    combine(plane_of(2))
    combine(plane_of(3))

    for plane in range(PLANES):
        for g, other in CARRIED:
            @pl.when((plane <= z) & (z < PLANES - 1))
            def _():
                up(plane, g, other).wait_send()

            @pl.when((plane >= z) & (z > 0))
            def _():
                down(plane, g, other).wait_send()

    over_x(z, 0, 0).wait_send()
    relayed(z, 0).wait_send()
    for g in range(1, GROUPS):
        over_x(z, g, 0).wait_send()
        over_x(z, g, 1).wait_send()
    for k in (1, 2, 3):
        for g in range(GROUPS):
            over_x(plane_of(k), g, 0).wait_send()
            relayed(plane_of(k), g).wait_send()
            if g < SINGLE:
                over_y(plane_of(k), g).wait_send()
    for plane in range(PLANES):
        give(plane).wait()


def per_device_kernel(train_codes, block_scales, queries, left_factor, right_factor):
    rows, _, width = train_codes.shape
    count = queries.shape[0]
    order = left_factor.shape[1]
    step = count // GROUPS
    blocks = block_scales.shape[2]
    total = 2 * PLANES * count
    hbm = pl.BlockSpec(memory_space=pl.ANY)
    return pl.pallas_call(
        score_kernel,
        out_shape=jax.ShapeDtypeStruct((rows // 2, total), jnp.float32),
        in_specs=[hbm] * 5,
        out_specs=hbm,
        scratch_shapes=[
            pltpu.VMEM((rows, width), jnp.bfloat16),
            pltpu.VMEM((rows, width), jnp.bfloat16),
            pltpu.VMEM((blocks, rows), jnp.float32),
            pltpu.VMEM((rows, blocks), jnp.float32),
            pltpu.VMEM((count, width), jnp.bfloat16),
            pltpu.VMEM((order, order), jnp.float32),
            pltpu.VMEM((order, order), jnp.float32),
            pltpu.VMEM((total, width), jnp.bfloat16),
            pltpu.VMEM((step * order, 128), jnp.float32),
            pltpu.VMEM((step * order, 128), jnp.float32),
            pltpu.VMEM((2, 4 * order, 4 * order), jnp.bfloat16),
            pltpu.VMEM((2, 4 * order, 4 * order), jnp.bfloat16),
            pltpu.VMEM((PLANES, 2, rows // 2, 2 * count), jnp.float32),
            pltpu.VMEM((PLANES, rows // 2, 2 * count), jnp.float32),
            pltpu.VMEM((PLANES, rows // 2, 2 * count), jnp.float32),
            pltpu.SemaphoreType.DMA((4,)),
            pltpu.SemaphoreType.DMA((GROUPS,)),
            pltpu.SemaphoreType.DMA((PLANES,)),
            pltpu.SemaphoreType.DMA((2 * PLANES, 2 * GROUPS)),
            pltpu.SemaphoreType.DMA((PLANES, 2 * GROUPS)),
            pltpu.SemaphoreType.DMA((PLANES, 2 * GROUPS)),
            pltpu.SemaphoreType.DMA((PLANES, 2 * GROUPS)),
            pltpu.SemaphoreType.DMA((PLANES, GROUPS)),
            pltpu.SemaphoreType.DMA((PLANES, GROUPS)),
            pltpu.SemaphoreType.DMA((PLANES,)),
            pltpu.SemaphoreType.DMA((PLANES,)),
        ],
        compiler_params=pltpu.CompilerParams(
            collective_id=0, has_side_effects=True, vmem_limit_bytes=60 * 1024 * 1024
        ),
        cost_estimate=pl.CostEstimate(
            flops=2 * rows * total * width, bytes_accessed=2 * rows * width, transcendentals=0
        ),
        name="score_kernel",
    )(
        train_codes.reshape(rows, width),
        block_scales.reshape(rows, blocks).T,
        queries.reshape(count, width),
        left_factor.reshape(order, order),
        right_factor.reshape(order, order),
    )


def precondition(flat, left_factor, right_factor):
    count = flat.shape[0]
    layers = left_factor.shape[0]
    outer = left_factor.shape[1]
    inner = right_factor.shape[1]
    blocks = flat.reshape(count, layers, outer, inner).astype(jnp.float32)
    result = jnp.einsum(
        "lab,nlbc,lcd->nlad", left_factor, blocks, right_factor, precision=lax.Precision.HIGHEST
    )
    return result.astype(jnp.bfloat16).reshape(count, layers * outer * inner)


def per_device(train_codes, block_scales, queries, left_factor, right_factor):
    rows, layers, width = train_codes.shape
    blocks = block_scales.shape[2]
    values = (
        train_codes.reshape(rows, layers, blocks, width // blocks).astype(jnp.float32)
        * block_scales[..., None]
    )
    dequant = values.astype(jnp.bfloat16).reshape(rows, layers * width)
    flat = queries.reshape(queries.shape[0], layers * width)
    sending = precondition(flat, left_factor, right_factor)
    partial_scores = jnp.einsum(
        "rk,qk->rq",
        dequant,
        lax.all_gather(sending, "row", axis=0, tiled=True),
        preferred_element_type=jnp.float32,
    )
    return lax.psum_scatter(partial_scores, "layer", scatter_dimension=0, tiled=True)


def solution(mesh):
    small = mesh.shape["grp"] == 2 and mesh.shape["row"] == 2 * PLANES and mesh.shape["layer"] == 2
    return jax.shard_map(
        per_device_kernel if small else per_device,
        mesh=mesh,
        in_specs=(
            P(("grp", "row"), "layer", None),
            P(("grp", "row"), "layer", None),
            P("row", "layer", None),
            P("layer", None, None),
            P("layer", None, None),
        ),
        out_specs=P(("grp", "row", "layer"), None),
        check_vma=False,
    )
```

```python
import jax
import jax.numpy as jnp
from jax import lax
from jax.experimental import pallas as pl
from jax.experimental.pallas import tpu as pltpu
from jax.sharding import PartitionSpec as P

MESH = pl.DeviceIdType.MESH
PLANES = 4
GROUPS = 4
SINGLE = 2
LAG = 3
AHEAD = 4
CARRIED = [(g, other) for other in range(2) for g in range(GROUPS) if not (other and g < SINGLE)]


def split(value):
    high = value.astype(jnp.bfloat16)
    return high, (value - high.astype(jnp.float32)).astype(jnp.bfloat16)


def dot(a, b):
    return jnp.dot(a, b, preferred_element_type=jnp.float32)


def score_kernel(
    codes_hbm, scales_hbm, queries_hbm, left_hbm, right_hbm, out_hbm,
    codes, train, flat_scales, scales, queries, left, right, prepared, spread, mixed,
    left_diag, right_diag, mine, theirs, result,
    fetch_sem, query_sem, out_sem, recv_sem, up_sem, down_sem, x_sem, relay_sem, y_sem, part_sem, part_recv_sem,
):
    rows, width = codes.shape
    order = left.shape[0]
    count = queries.shape[0]
    step = count // GROUPS
    half = rows // 2
    y, at, layer = lax.axis_index("grp"), lax.axis_index("row"), lax.axis_index("layer")
    z, x = at // 2, at % 2
    middle = (z * (PLANES - 1 - z)) // 2
    sign = 1 - 2 * (z // 2)
    above = {"row": at + 2}
    below = {"row": at - 2}
    beside = {"row": at + 1 - 2 * x}
    across = {"grp": 1 - y}
    core = {"layer": 1 - layer}

    barrier = pltpu.get_barrier_semaphore()
    for where in (beside, across, core):
        pl.semaphore_signal(barrier, inc=1, device_id=where, device_id_type=MESH)

    @pl.when(z > 0)
    def _():
        pl.semaphore_signal(barrier, inc=1, device_id=below, device_id_type=MESH)

    @pl.when(z < PLANES - 1)
    def _():
        pl.semaphore_signal(barrier, inc=1, device_id=above, device_id_type=MESH)

    def fetch_queries(g):
        span = pl.ds(g * step, step)
        return pltpu.make_async_copy(queries_hbm.at[span, :], queries.at[span, :], query_sem.at[g])

    fetch_left = pltpu.make_async_copy(left_hbm, left, fetch_sem.at[0])
    fetch_right = pltpu.make_async_copy(right_hbm, right, fetch_sem.at[1])
    fetch_scales = pltpu.make_async_copy(scales_hbm, flat_scales, fetch_sem.at[2])
    fetch_codes = pltpu.make_async_copy(codes_hbm, codes, fetch_sem.at[3])
    fetch_right.start()
    fetch_left.start()
    for g in range(GROUPS):
        fetch_queries(g).start()
    fetch_scales.start()
    fetch_codes.start()

    def plane_of(k):
        step_middle = (1, -1, 2)[k - 1]
        return z + sign * (k + middle * (step_middle - k))

    def half_of(other):
        return y + other * (1 - 2 * y)

    def piece(plane, side, g, h):
        start = pl.multiple_of((plane * 2 + side) * count + g * step, step)
        return prepared.at[pl.ds(start, step), pl.ds(pl.multiple_of(h * (width // 2), width // 2), width // 2)]

    def hop(plane, side, g, other, send_sem, where):
        h = half_of(other)
        block = piece(plane, side, g, h)
        return pltpu.make_async_remote_copy(
            src_ref=block, dst_ref=block, send_sem=send_sem, recv_sem=recv_sem.at[plane * 2 + side, 2 * g + h],
            device_id=where, device_id_type=MESH,
        )

    def up(plane, g, other):
        return hop(plane, x, g, other, up_sem.at[plane, 2 * g + other], above)

    def down(plane, g, other):
        return hop(plane, x, g, other, down_sem.at[plane, 2 * g + other], below)

    def over_x(plane, g, other):
        return hop(plane, x, g, other, x_sem.at[plane, 2 * g + other], beside)

    def over_y(plane, g):
        return hop(plane, x, g, 0, y_sem.at[plane, g], across)

    def relayed(plane, g):
        return hop(plane, 1 - x, g, 0, relay_sem.at[plane, g], across)

    def landed(plane, side, g, other):
        hop(plane, side, g, other, up_sem.at[0, 0], beside).wait_recv()

    def fill_diag(ref, diag):
        tall = jnp.concatenate([ref[...]] * 4, axis=0)
        wide = jnp.concatenate([jnp.concatenate([tall, tall], axis=1)] * 2, axis=1)
        row_at = lax.broadcasted_iota(jnp.int32, wide.shape, 0) // order
        col_at = lax.broadcasted_iota(jnp.int32, wide.shape, 1) // order
        high, low = split(jnp.where(row_at == col_at, wide, 0.0))
        diag[0] = high
        diag[1] = low

    lane = lax.broadcasted_iota(jnp.int32, (step, 128), 1)

    def prepare(c):
        fetch_queries(c).wait()
        piece_of = queries[c * step : (c + 1) * step, :]
        stacked = jnp.concatenate([piece_of[:, g * 256 : (g + 1) * 256] for g in range(width // 256)], axis=0)
        turned = dot(stacked, right_diag[0]) + dot(stacked, right_diag[1])
        for pair in range(width // 128):
            g, h = pair // 2, pair % 2
            value = turned[g * step : (g + 1) * step, h * 128 : (h + 1) * 128]
            spread[pl.ds(2 * pair, step, stride=order), :] = value
            spread[pl.ds(2 * pair + 1, step, stride=order), :] = pltpu.roll(value, 64, 1)
        for i in range(step // 4):
            high, low = split(spread[i * 256 : (i + 1) * 256, :])
            mixed[i * 256 : (i + 1) * 256, :] = (
                dot(left_diag[0], high) + dot(left_diag[1], high) + dot(left_diag[0], low)
            )
        start = pl.multiple_of(at * count + c * step, step)
        for pair in range(width // 128):
            even = mixed[pl.ds(2 * pair, step, stride=order), :]
            odd = pltpu.roll(mixed[pl.ds(2 * pair + 1, step, stride=order), :], 64, 1)
            prepared[pl.ds(start, step), pair * 128 : (pair + 1) * 128] = jnp.where(
                lane < 64, even, odd
            ).astype(jnp.bfloat16)

    def relay(plane, g):
        landed(plane, 1 - x, g, 0)
        relayed(plane, g).start()

    def finish_own():
        landed(z, 1 - x, 0, 1)
        for g in range(1, GROUPS):
            landed(z, 1 - x, g, 0)
            landed(z, 1 - x, g, 1)

    def finish(plane):
        for g in range(GROUPS):
            if g < SINGLE:
                landed(plane, x, g, 1)
            landed(plane, 1 - x, g, 1)

    def exchange(plane):
        return pltpu.make_async_remote_copy(
            src_ref=mine.at[plane, 1 - layer], dst_ref=theirs.at[plane],
            send_sem=part_sem.at[plane], recv_sem=part_recv_sem.at[plane],
            device_id=core, device_id_type=MESH,
        )

    def score(plane):
        start = pl.multiple_of(plane * 2 * count, 2 * count)
        for h in range(2):
            mine[plane, h] = lax.dot_general(
                train[h * half : (h + 1) * half, :], prepared[pl.ds(start, 2 * count), :],
                (((1,), (1,)), ((), ())), preferred_element_type=jnp.float32,
            )
        exchange(plane).start()

    def give(plane):
        start = pl.multiple_of(plane * 2 * count, 2 * count)
        return pltpu.make_async_copy(result.at[plane], out_hbm.at[:, pl.ds(start, 2 * count)], out_sem.at[plane])

    def combine(plane):
        exchange(plane).wait()
        result[plane] = mine[plane, layer] + theirs[plane]
        give(plane).start()

    def dequantize(part):
        @pl.loop(0, rows // (64 * GROUPS))
        def _(t):
            span = pl.ds(pl.multiple_of(part * (rows // GROUPS) + t * 64, 64), 64)
            for j in range(width // 128):
                train[span, j * 128 : (j + 1) * 128] = (
                    codes[span, j * 128 : (j + 1) * 128].astype(jnp.float32) * scales[span, j : j + 1]
                ).astype(jnp.bfloat16)

    fetch_right.wait()
    fill_diag(right, right_diag)
    fetch_left.wait()
    fill_diag(left, left_diag)
    def send_own(g, other):
        @pl.when(z < PLANES - 1)
        def _():
            up(z, g, other).start()

        @pl.when(z > 0)
        def _():
            down(z, g, other).start()

    def outward(plane, g, other):
        @pl.when(z == 1)
        def _():
            down(plane, g, other).start()

        @pl.when(z == 2)
        def _():
            up(plane, g, other).start()

    def inward(plane, g, other):
        @pl.when(z == 1)
        def _():
            up(plane, g, other).start()

        @pl.when(z == 2)
        def _():
            down(plane, g, other).start()

    later = []
    for g in range(GROUPS):
        prepare(g)
        if g == 0:
            pl.semaphore_wait(barrier, 3 + jnp.minimum(z, 1) + jnp.minimum(PLANES - 1 - z, 1))
        for row_group, other in CARRIED[:AHEAD]:
            if row_group == g:
                send_own(g, other)
        if g == 0:
            over_x(z, 0, 0).start()
        elif g == 1:
            over_x(z, 1, 0).start()
            over_x(z, 1, 1).start()
        else:
            later += [(g, 0), (g, 1)]

    fetch_scales.wait()
    scales[...] = flat_scales[...].T
    fetch_codes.wait()
    relay(z, 0)

    events = [(k, g, other) for k in (1, 2, 3) for g, other in CARRIED]
    relays = {}
    for e, (k, g, other) in enumerate(events):
        if not other:
            relays.setdefault(e + LAG, []).append((k, g))
    for e, (k, g, other) in enumerate(events):
        plane = plane_of(k)
        if k == 1:
            landed(plane, x, g, other)
        else:
            @pl.when(middle == 0)
            def _():
                landed(plane, x, g, other)

        due = e + AHEAD
        each = len(CARRIED)
        if due < each:
            send_own(*CARRIED[due])
        elif due < 2 * each:
            due_piece = CARRIED[due - each]

            @pl.when(middle == 1)
            def _():
                outward(plane_of(1), *due_piece)
                landed(plane_of(2), x, *due_piece)
                inward(plane_of(2), *due_piece)
        elif due < 3 * each:
            due_piece = CARRIED[due - 2 * each]

            @pl.when(middle == 1)
            def _():
                landed(plane_of(3), x, *due_piece)
                outward(plane_of(3), *due_piece)

        if other:
            if later:
                over_x(z, *later.pop(0)).start()
        else:
            over_x(plane, g, 0).start()
            if g < SINGLE:
                over_y(plane, g).start()
        for late_k, late_g in relays.pop(e, []):
            relay(plane_of(late_k), late_g)
        if e in (1, 3, 5, 7):
            dequantize(e // 2)
        if e == 13:
            finish_own()
            score(z)
        if e == 15:
            finish(plane_of(1))
            score(plane_of(1))
    for e in sorted(relays):
        for late_k, late_g in relays[e]:
            relay(plane_of(late_k), late_g)
    finish(plane_of(2))
    score(plane_of(2))
    combine(z)
    combine(plane_of(1))
    finish(plane_of(3))
    score(plane_of(3))
    combine(plane_of(2))
    combine(plane_of(3))

    for plane in range(PLANES):
        for g, other in CARRIED:
            @pl.when((plane <= z) & (z < PLANES - 1))
            def _():
                up(plane, g, other).wait_send()

            @pl.when((plane >= z) & (z > 0))
            def _():
                down(plane, g, other).wait_send()

    over_x(z, 0, 0).wait_send()
    relayed(z, 0).wait_send()
    for g in range(1, GROUPS):
        over_x(z, g, 0).wait_send()
        over_x(z, g, 1).wait_send()
    for k in (1, 2, 3):
        for g in range(GROUPS):
            over_x(plane_of(k), g, 0).wait_send()
            relayed(plane_of(k), g).wait_send()
            if g < SINGLE:
                over_y(plane_of(k), g).wait_send()
    for plane in range(PLANES):
        give(plane).wait()


def per_device_kernel(train_codes, block_scales, queries, left_factor, right_factor):
    rows, _, width = train_codes.shape
    count = queries.shape[0]
    order = left_factor.shape[1]
    step = count // GROUPS
    blocks = block_scales.shape[2]
    total = 2 * PLANES * count
    hbm = pl.BlockSpec(memory_space=pl.ANY)
    return pl.pallas_call(
        score_kernel,
        out_shape=jax.ShapeDtypeStruct((rows // 2, total), jnp.float32),
        in_specs=[hbm] * 5,
        out_specs=hbm,
        scratch_shapes=[
            pltpu.VMEM((rows, width), jnp.bfloat16),
            pltpu.VMEM((rows, width), jnp.bfloat16),
            pltpu.VMEM((blocks, rows), jnp.float32),
            pltpu.VMEM((rows, blocks), jnp.float32),
            pltpu.VMEM((count, width), jnp.bfloat16),
            pltpu.VMEM((order, order), jnp.float32),
            pltpu.VMEM((order, order), jnp.float32),
            pltpu.VMEM((total, width), jnp.bfloat16),
            pltpu.VMEM((step * order, 128), jnp.float32),
            pltpu.VMEM((step * order, 128), jnp.float32),
            pltpu.VMEM((2, 4 * order, 4 * order), jnp.bfloat16),
            pltpu.VMEM((2, 4 * order, 4 * order), jnp.bfloat16),
            pltpu.VMEM((PLANES, 2, rows // 2, 2 * count), jnp.float32),
            pltpu.VMEM((PLANES, rows // 2, 2 * count), jnp.float32),
            pltpu.VMEM((PLANES, rows // 2, 2 * count), jnp.float32),
            pltpu.SemaphoreType.DMA((4,)),
            pltpu.SemaphoreType.DMA((GROUPS,)),
            pltpu.SemaphoreType.DMA((PLANES,)),
            pltpu.SemaphoreType.DMA((2 * PLANES, 2 * GROUPS)),
            pltpu.SemaphoreType.DMA((PLANES, 2 * GROUPS)),
            pltpu.SemaphoreType.DMA((PLANES, 2 * GROUPS)),
            pltpu.SemaphoreType.DMA((PLANES, 2 * GROUPS)),
            pltpu.SemaphoreType.DMA((PLANES, GROUPS)),
            pltpu.SemaphoreType.DMA((PLANES, GROUPS)),
            pltpu.SemaphoreType.DMA((PLANES,)),
            pltpu.SemaphoreType.DMA((PLANES,)),
        ],
        compiler_params=pltpu.CompilerParams(
            collective_id=0, has_side_effects=True, vmem_limit_bytes=60 * 1024 * 1024
        ),
        cost_estimate=pl.CostEstimate(
            flops=2 * rows * total * width, bytes_accessed=2 * rows * width, transcendentals=0
        ),
        name="score_kernel",
    )(
        train_codes.reshape(rows, width),
        block_scales.reshape(rows, blocks).T,
        queries.reshape(count, width),
        left_factor.reshape(order, order),
        right_factor.reshape(order, order),
    )


def precondition(flat, left_factor, right_factor):
    count = flat.shape[0]
    layers = left_factor.shape[0]
    outer = left_factor.shape[1]
    inner = right_factor.shape[1]
    blocks = flat.reshape(count, layers, outer, inner).astype(jnp.float32)
    result = jnp.einsum(
        "lab,nlbc,lcd->nlad", left_factor, blocks, right_factor, precision=lax.Precision.HIGHEST
    )
    return result.astype(jnp.bfloat16).reshape(count, layers * outer * inner)


def per_device(train_codes, block_scales, queries, left_factor, right_factor):
    rows, layers, width = train_codes.shape
    blocks = block_scales.shape[2]
    values = (
        train_codes.reshape(rows, layers, blocks, width // blocks).astype(jnp.float32)
        * block_scales[..., None]
    )
    dequant = values.astype(jnp.bfloat16).reshape(rows, layers * width)
    flat = queries.reshape(queries.shape[0], layers * width)
    sending = precondition(flat, left_factor, right_factor)
    partial_scores = jnp.einsum(
        "rk,qk->rq",
        dequant,
        lax.all_gather(sending, "row", axis=0, tiled=True),
        preferred_element_type=jnp.float32,
    )
    return lax.psum_scatter(partial_scores, "layer", scatter_dimension=0, tiled=True)


def solution(mesh):
    small = mesh.shape["grp"] == 2 and mesh.shape["row"] == 2 * PLANES and mesh.shape["layer"] == 2
    return jax.shard_map(
        per_device_kernel if small else per_device,
        mesh=mesh,
        in_specs=(
            P(("grp", "row"), "layer", None),
            P(("grp", "row"), "layer", None),
            P("row", "layer", None),
            P("layer", None, None),
            P("layer", None, None),
        ),
        out_specs=P(("grp", "row", "layer"), None),
        check_vma=False,
    )
```
